256 devices in a mesh: docs: 32 (over z, y_lo, core), layer: 8 (over y_hi, x).
Axes of the slice: x: 4, y: 4 (y_hi: 2, y_lo: 2; y = y_hi * 2 + y_lo), z: 8, core: 2. Of those that a mesh axis runs over, the one named last changes fastest.
Arguments:
- grad_out: bfloat16 [3584, 8, 32, 256], P('docs', 'layer')
- acts: bfloat16 [3584, 8, 256, 128], P('docs', 'layer')
- lengths: int32 [3584], P('docs'), may hold values from 64 to 256
Outputs:
- kernel: float32 [3584, 3584], P('docs', 'layer')
The draws below stay inside these ranges and needn't reach their ends.
All inputs are finite; a program needn't handle non-finite values.
Results may differ from the reference program's by a relative error of at most 0.00064.
Values may be sent and summed in bfloat16 or wider, within the bound.
A program may use at most 128 MiB of HBM per device.

```python
import jax
import jax.numpy as jnp
from jax import lax

KO = 32
KI = 128
DB = 112
SEQ = 256
LAYERS = 8
DOCS = 3584


def draw_grad_out(key, part):
    key = jax.random.fold_in(key, 23)
    first, second, third = jax.random.split(key, 3)
    base = jax.random.normal(first, (1, LAYERS, KO, 1), jnp.float32)
    shape = (DOCS, LAYERS, KO, SEQ)
    steps = jnp.arange(LAYERS, dtype=jnp.float32) / max(LAYERS - 1, 1)
    amount = jax.random.uniform(second, (DOCS, LAYERS, 1, 1), jnp.float32, -1.5, 1.5)
    noise = jax.random.normal(third, shape, jnp.float32)
    layer_ramp = 1.0 + 2.0 * steps
    ramp = 1.0 + 2.0 * jnp.arange(KO, dtype=jnp.float32) / (KO - 1)
    scaled = (amount * base + noise) * ramp[None, None, :, None] * layer_ramp[None, :, None, None]
    return scaled.astype(jnp.bfloat16)


def draw_acts(key, part):
    key = jax.random.fold_in(key, 11)
    first, second = jax.random.split(key, 2)
    shape = (DOCS, LAYERS, SEQ, KI)
    base = jax.random.normal(first, (1, LAYERS, SEQ, KI), jnp.float32)
    noise = jax.random.normal(second, shape, jnp.float32)
    return (0.8 * base + noise).astype(jnp.bfloat16)


def with_ends(result, own_key, smallest, high):
    index_at = [jax.random.randint(jax.random.fold_in(own_key, axis), (), 0, length) for axis, length in enumerate(result.shape)]
    longest = result.shape.index(max(result.shape))
    next_to = index_at[:longest] + [(index_at[longest] + 1) % result.shape[longest]] + index_at[longest + 1:]
    return result.at[tuple(index_at)].set(smallest).at[tuple(next_to)].set(high)


def setup_inputs(seed: int = 0) -> dict:
    seeds = jax.random.split(jax.random.key(seed), 4)
    grad_out = draw_grad_out(jax.random.fold_in(seeds[3], 71), 0)
    acts = draw_acts(jax.random.fold_in(seeds[3], 71), 0)
    lengths = with_ends(jax.random.randint(seeds[2], (DOCS,), SEQ // 4, SEQ + 1), jax.random.fold_in(seeds[2], 1), SEQ // 4, SEQ).astype(jnp.int32)
    return dict(grad_out=grad_out, acts=acts, lengths=lengths)


def block_features(items):
    grads, inputs, counts = items
    slots = lax.broadcasted_iota(jnp.int32, (counts.shape[0], inputs.shape[2]), 1)
    valid = (slots < counts[:, None]).astype(jnp.float32)
    masked = inputs.astype(jnp.float32) * valid[:, None, :, None]
    summed = jnp.einsum('dlot,dlti->dloi', grads.astype(jnp.float32), masked)
    return summed.reshape(summed.shape[0], LAYERS * KO * KI)

def reference(grad_out, acts, lengths):
    blocks = DOCS // DB
    feature = lax.map(block_features, (grad_out.reshape(blocks, DB, LAYERS, KO, SEQ), acts.reshape(blocks, DB, LAYERS, SEQ, KI), lengths.reshape(blocks, DB)))
    feature = feature.reshape(DOCS, LAYERS * KO * KI)
    squares = lax.optimization_barrier(jnp.sum(feature * feature, axis=1))
    unit = (feature * lax.rsqrt(squares + 1e-06)[:, None]).astype(jnp.bfloat16)
    wide = unit.astype(jnp.float32)
    return jnp.dot(wide, wide.T, precision=lax.Precision.HIGHEST)
```

```python
import functools

import jax
import jax.numpy as jnp
from jax import lax
from jax.experimental import pallas as pl
from jax.experimental.pallas import tpu as pltpu
from jax.sharding import PartitionSpec as P

epsilon = 1e-06
MESH = pl.DeviceIdType.MESH
F32 = jnp.float32
BF16 = jnp.bfloat16

DB = 112
KO = 32
KI = 128
SEQ = 256
NZ = 8
CH = 16
GO = 8
PR = 56


def body(
    lengths_ref, grad_hbm, acts_hbm, out_ref,
    gbuf, abuf, feat, S, R, PP, RR, V, L, T, sq, sqr,
    in_sem, qs, qr, zs, zr, ys, yr, cs, cr, rs, rr, ls, ts, lr, tr,
):
    d = lax.axis_index("docs")
    me_l = lax.axis_index("layer")
    z, yl, c = d // 4, (d // 2) % 2, d % 2
    me = yl * 2 + c
    yme = (1 - yl) * 2 + c

    def dev(zz, slot, ll):
        return (zz * 4 + slot, ll)

    up = dev(lax.rem(z + 1, NZ), me, me_l)
    down = dev(lax.rem(z + NZ - 1, NZ), me, me_l)
    ypart = dev(z, yme, me_l)
    cpart = dev(z, yl * 2 + 1 - c, me_l)
    self_final = (me_l // 2) == me

    def rcopy(src, dst, ss, rs_, to):
        return pltpu.make_async_remote_copy(
            src_ref=src, dst_ref=dst, send_sem=ss, recv_sem=rs_, device_id=to, device_id_type=MESH
        )

    chunks = DB // CH
    def in_copies(k):
        rows = pl.ds(k * CH, CH)
        return (
            pltpu.make_async_copy(grad_hbm.at[rows], gbuf.at[rows], in_sem.at[0, k]),
            pltpu.make_async_copy(acts_hbm.at[rows], abuf.at[rows], in_sem.at[1, k]),
        )
    for k in range(chunks):
        for copy in in_copies(k):
            copy.start()

    barrier = pltpu.get_barrier_semaphore()
    def hello(to):
        pl.semaphore_signal(barrier, inc=1, device_id=to, device_id_type=MESH)
    for to in (up, down, ypart, cpart):
        hello(to)
    @pl.loop(1, NZ)
    def _(p):
        hello(dev(z, me, lax.rem(me_l + p, NZ)))
    @pl.loop(0, 8)
    def _(i):
        ll = 2 * me + i // 4
        slot = i % 4
        @pl.when(jnp.logical_not((ll == me_l) & (slot == me)))
        def _():
            hello(dev(z, slot, ll))
    @pl.when(me_l != z)
    def _():
        @pl.loop(0, NZ)
        def _(g):
            hello(dev(me_l, me, g))

    @pl.loop(0, chunks)
    def _(k):
        for copy in in_copies(k):
            copy.wait()
        @pl.loop(0, CH, unroll=4)
        def _(j):
            doc = k * CH + j
            n = lengths_ref[doc]
            slots = lax.broadcasted_iota(jnp.int32, (KO, SEQ), 1)
            valid = (slots < n).astype(F32).astype(BF16)
            feat[pl.ds(pl.multiple_of(doc * KO, KO), KO), :] = jnp.dot(
                gbuf[doc] * valid, abuf[doc], preferred_element_type=F32
            )

    acc = jnp.zeros((DB, KI), F32)
    for o in range(KO):
        x = feat[pl.ds(o, DB, stride=KO), :]
        acc = acc + x * x
    eye = lax.broadcasted_iota(jnp.int32, (DB, KI), 0) == lax.broadcasted_iota(jnp.int32, (DB, KI), 1)
    col = jnp.broadcast_to(jnp.sum(acc, axis=1, keepdims=True), (DB, KI))
    row = jnp.sum(jnp.where(eye, col, 0.0), axis=0, keepdims=True)
    sq[...] = jnp.broadcast_to(row, (8, KI))

    pl.semaphore_wait(barrier, 4 + 7 + 8 + 7 - self_final.astype(jnp.int32))

    def sq_copy(p):
        return rcopy(sq, sqr.at[p - 1], qs.at[p - 1], qr.at[p - 1], dev(z, me, lax.rem(me_l + p, NZ)))
    @pl.loop(1, NZ)
    def _(p):
        sq_copy(p).start()
    PP[...] = jnp.zeros_like(PP)
    @pl.when(me_l == z)
    def _():
        T[...] = jnp.zeros_like(T)
    @pl.loop(1, NZ)
    def _(p):
        sq_copy(p).wait()
    total = sq[0:1, :]
    for p in range(NZ - 1):
        total = total + sqr[p, 0:1, :]
    scale = jnp.sum(jnp.where(eye, jnp.broadcast_to(total, (DB, KI)), 0.0), axis=1, keepdims=True)
    scale = jnp.broadcast_to(lax.rsqrt(scale + epsilon), (DB, KI))

    def slot_of(h, sub, direction):
        return (h - 1) * 4 + sub * 2 + direction

    def z_copy(h, sub, direction):
        kc = direction * 2 + sub
        src = S.at[kc, me] if h == 1 else R.at[slot_of(h - 1, sub, direction)]
        to = (up, down)[direction]
        if h == 4:
            return rcopy(src, R.at[12 + direction], zs.at[direction, 3, 0], zr.at[direction, 3, 0], to)
        return rcopy(
            src, R.at[slot_of(h, sub, direction)], zs.at[direction, h - 1, sub], zr.at[direction, h - 1, sub], to
        )

    def y_copy(kc):
        return rcopy(S.at[kc, me], S.at[kc, me], ys.at[kc], yr.at[kc], ypart)

    def c_copy(which, kc):
        slot = (me, yme)[which]
        return rcopy(S.at[kc, slot], S.at[kc, slot], cs.at[which, kc], cr.at[which, kc], cpart)

    order = (0, 2, 1, 3)
    for kc in order:
        for j in range(GO):
            x = feat[pl.ds(kc * GO + j, DB, stride=KO), :]
            S[kc, me, j] = (x * scale).astype(BF16)
        z_copy(1, kc % 2, kc // 2).start()
        y_copy(kc).start()
        c_copy(0, kc).start()

    def product(kc, xs):
        right = jnp.concatenate([xs[j] for j in range(GO)], axis=1)
        right = jnp.concatenate([right, jnp.zeros((KI - DB, GO * KI), BF16)], axis=0)
        left = jnp.concatenate(
            [jnp.concatenate([S[kc, r, j] for j in range(GO)], axis=1) for r in range(4)], axis=0
        )
        res = lax.dot_general(left, right, (((1,), (1,)), ((), ())), preferred_element_type=F32)
        return res.reshape(8, PR, KI)

    def multiply(i):
        h1, sub, direction = i // 4, (i // 2) % 2, i % 2
        PP[2 * h1 + direction] += product(direction * 2 + sub, R.at[i])

    def r_copy(b, p):
        to = lax.rem(me_l + p, NZ)
        return rcopy(PP.at[b, to], RR.at[b, p - 1], rs.at[b, p - 1], rr.at[b, p - 1], dev(z, me, to))

    def send_partials(b):
        @pl.loop(1, NZ)
        def _(p):
            r_copy(b, p).start()

    def plane_of(b):
        h = b // 2 + 1
        other = jnp.where(b % 2 == 0, z + NZ - h, z + h)
        return lax.rem(jnp.where(b == 7, z, jnp.where(b == 6, z + 4, other)), NZ)

    def l_copy(b):
        return rcopy(V.at[b], L.at[me, me_l % 2], ls.at[b], lr.at[me, me_l % 2], dev(z, me_l // 2, plane_of(b)))

    def l_copy_self(b):
        return pltpu.make_async_copy(V.at[b], L.at[me, me_l % 2], lr.at[me, me_l % 2])

    def t_copy(b):
        return rcopy(V.at[b], T.at[me_l], ts.at[b], tr.at[me_l], dev(plane_of(b), me, z))

    def finish(b):
        total = PP[b, me_l]
        for p in range(1, NZ):
            r_copy(b, p).wait_recv()
            total = total + RR[b, p - 1]
        V[b] = total
        to_self = self_final & (plane_of(b) == me_l)
        @pl.when(to_self)
        def _():
            l_copy_self(b).start()
        @pl.when(jnp.logical_not(to_self))
        def _():
            l_copy(b).start()
        @pl.when(b != 7)
        def _():
            t_copy(b).start()

    far = (lax.rem(z + NZ - 3, NZ) // 4, lax.rem(z + 3, NZ) // 4)
    arriving = lax.rem(z + 4, NZ) // 4

    for tick in range(6):
        h, sub = tick // 2 + 1, tick % 2
        for direction in range(2):
            z_copy(h, sub, direction).wait_recv()
            if h < 3:
                z_copy(h + 1, sub, direction).start()
            else:
                @pl.when(far[direction] == sub)
                def _():
                    z_copy(4, sub, direction).start()
        if tick < 4:
            kc = order[tick]
            y_copy(kc).wait_recv()
            c_copy(1, kc).start()
        if 1 <= tick <= 4:
            kc = order[tick - 1]
            c_copy(0, kc).wait_recv()
            c_copy(1, kc).wait_recv()
            PP[7] += product(kc, S.at[kc, me])
        if tick == 4:
            send_partials(7)
            @pl.loop(0, 8)
            def _(i):
                multiply(i)
            @pl.loop(0, 4)
            def _(b):
                send_partials(b)
            @pl.loop(8, 10)
            def _(i):
                multiply(i)
        if tick == 5:
            @pl.loop(10, 12)
            def _(i):
                multiply(i)
            @pl.loop(4, 6)
            def _(b):
                send_partials(b)

    finish(7)
    @pl.loop(0, 4)
    def _(b):
        finish(b)

    for direction in range(2):
        z_copy(4, 0, direction).wait_recv()
        PP[6] += product(direction * 2 + arriving, R.at[12 + direction])
    send_partials(6)
    @pl.loop(4, 7)
    def _(b):
        finish(b)

    for h in range(1, 5):
        for sub in range(2 if h < 4 else 1):
            for direction in range(2):
                z_copy(h, sub, direction).wait_send()
    for kc in range(4):
        y_copy(kc).wait_send()
        c_copy(0, kc).wait_send()
        c_copy(1, kc).wait_send()
    @pl.loop(0, 8)
    def _(b):
        @pl.loop(1, NZ)
        def _(p):
            r_copy(b, p).wait_send()
        to_self = self_final & (plane_of(b) == me_l)
        @pl.when(jnp.logical_not(to_self))
        def _():
            l_copy(b).wait_send()
        @pl.when(b != 7)
        def _():
            t_copy(b).wait_send()

    for t in range(4):
        for half in range(2):
            rcopy(V.at[0], L.at[t, half], ls.at[0], lr.at[t, half], up).wait_recv()
    @pl.when(me_l != z)
    def _():
        for g in range(NZ):
            rcopy(V.at[0], T.at[g], ts.at[0], tr.at[g], up).wait_recv()
    own = jnp.concatenate([L[t].reshape(DB, KI)[:, :DB] for t in range(4)], axis=1)
    other = jnp.transpose(T[...].reshape(NZ * PR, KI))
    out_ref[...] = own + other[:DB, :]


def local(grad_out, acts, lengths):
    grads = grad_out.reshape(DB, KO, SEQ)
    inputs = acts.reshape(DB, SEQ, KI)
    dma = pltpu.SemaphoreType.DMA
    return pl.pallas_call(
        body,
        out_shape=jax.ShapeDtypeStruct((DB, 4 * DB), F32),
        in_specs=[
            pl.BlockSpec(memory_space=pltpu.SMEM),
            pl.BlockSpec(memory_space=pl.ANY),
            pl.BlockSpec(memory_space=pl.ANY),
        ],
        out_specs=pl.BlockSpec(memory_space=pltpu.VMEM),
        scratch_shapes=[
            pltpu.VMEM((DB, KO, SEQ), BF16),
            pltpu.VMEM((DB, SEQ, KI), BF16),
            pltpu.VMEM((DB * KO, KI), F32),
            pltpu.VMEM((4, 4, GO, DB, KI), BF16),
            pltpu.VMEM((14, GO, DB, KI), BF16),
            pltpu.VMEM((8, 8, PR, KI), F32),
            pltpu.VMEM((8, 7, PR, KI), F32),
            pltpu.VMEM((8, PR, KI), F32),
            pltpu.VMEM((4, 2, PR, KI), F32),
            pltpu.VMEM((8, PR, KI), F32),
            pltpu.VMEM((8, KI), F32),
            pltpu.VMEM((7, 8, KI), F32),
            dma((2, DB // CH)),
            dma((7,)), dma((7,)),
            dma((2, 4, 2)), dma((2, 4, 2)),
            dma((4,)), dma((4,)),
            dma((2, 4)), dma((2, 4)),
            dma((8, 7)), dma((8, 7)),
            dma((8,)), dma((8,)),
            dma((4, 2)), dma((8,)),
        ],
        compiler_params=pltpu.CompilerParams(
            collective_id=0, has_side_effects=True, vmem_limit_bytes=48 * 2**20
        ),
    )(lengths, grads, inputs)


def solution(mesh):
    placed = (P("docs", "layer", None, None), P("docs", "layer", None, None), P("docs"))
    return jax.shard_map(
        local, mesh=mesh, in_specs=placed, out_specs=P("docs", "layer"), check_vma=False
    )
```

```python
import functools

import jax
import jax.numpy as jnp
from jax import lax
from jax.experimental import pallas as pl
from jax.experimental.pallas import tpu as pltpu
from jax.sharding import PartitionSpec as P

epsilon = 1e-06
MESH = pl.DeviceIdType.MESH
F32 = jnp.float32
BF16 = jnp.bfloat16

DB = 112
KO = 32
KI = 128
SEQ = 256
NZ = 8
CH = 16
GO = 8
PR = 56


def body(
    lengths_ref, grad_hbm, acts_hbm, out_ref,
    gbuf, abuf, feat, S, R, PP, RR, XS, RY, V, L, T, sq, sqr, norm, norms,
    in_sem, qs, qr, ns, nr, zs, zr, ys, yr, cs, cr, rs, rr, ps, pr, ls, ts, lr, tr,
):
    d = lax.axis_index("docs")
    me_l = lax.axis_index("layer")
    z, yl, c = d // 4, (d // 2) % 2, d % 2
    yh, x = me_l // 4, me_l % 4
    me = yl * 2 + c
    yme = (1 - yl) * 2 + c

    def dev(zz, slot, ll):
        return (zz * 4 + slot, ll)

    up = dev(lax.rem(z + 1, NZ), me, me_l)
    down = dev(lax.rem(z + NZ - 1, NZ), me, me_l)
    ypart = dev(z, yme, me_l)
    cpart = dev(z, yl * 2 + 1 - c, me_l)
    self_final = (me_l // 2) == me
    diagonal = me_l == z

    def rcopy(src, dst, ss, rs_, to):
        return pltpu.make_async_remote_copy(
            src_ref=src, dst_ref=dst, send_sem=ss, recv_sem=rs_, device_id=to, device_id_type=MESH
        )

    chunks = DB // CH
    def in_copies(k):
        rows = pl.ds(k * CH, CH)
        return (
            pltpu.make_async_copy(grad_hbm.at[rows], gbuf.at[rows], in_sem.at[0, k]),
            pltpu.make_async_copy(acts_hbm.at[rows], abuf.at[rows], in_sem.at[1, k]),
        )
    for k in range(chunks):
        for copy in in_copies(k):
            copy.start()

    barrier = pltpu.get_barrier_semaphore()
    def hello(to):
        pl.semaphore_signal(barrier, inc=1, device_id=to, device_id_type=MESH)
    for to in (up, down, ypart, cpart):
        hello(to)
    @pl.loop(1, NZ)
    def _(p):
        hello(dev(z, me, lax.rem(me_l + p, NZ)))
    @pl.loop(0, 8)
    def _(i):
        ll = 2 * me + i // 4
        slot = i % 4
        @pl.when(jnp.logical_not((ll == me_l) & (slot == me)))
        def _():
            hello(dev(z, slot, ll))
    @pl.when(jnp.logical_not(diagonal))
    def _():
        @pl.loop(0, NZ)
        def _(g):
            hello(dev(me_l, me, g))
    @pl.loop(0, 4)
    def _(t):
        @pl.when(jnp.logical_not(diagonal & (t == me)))
        def _():
            hello(dev(me_l, t, z))

    @pl.loop(0, chunks)
    def _(k):
        for copy in in_copies(k):
            copy.wait()
        @pl.loop(0, CH, unroll=CH)
        def _(j):
            doc = k * CH + j
            n = lengths_ref[doc]
            slots = lax.broadcasted_iota(jnp.int32, (KO, SEQ), 1)
            valid = (slots < n).astype(F32).astype(BF16)
            feat[pl.ds(pl.multiple_of(doc * KO, KO), KO), :] = jnp.dot(
                gbuf[doc] * valid, abuf[doc], preferred_element_type=F32
            )

    pl.semaphore_wait(barrier, 4 + 7 + 8 + 7 + 4 - self_final.astype(jnp.int32) - diagonal.astype(jnp.int32))

    def slot_of(h, sub, direction):
        return (h - 1) * 4 + sub * 2 + direction

    def z_copy(h, sub, direction):
        kc = direction * 2 + sub
        src = S.at[kc, me] if h == 1 else R.at[slot_of(h - 1, sub, direction)]
        to = (up, down)[direction]
        if h == 4:
            return rcopy(src, R.at[12 + direction], zs.at[direction, 3, 0], zr.at[direction, 3, 0], to)
        return rcopy(
            src, R.at[slot_of(h, sub, direction)], zs.at[direction, h - 1, sub], zr.at[direction, h - 1, sub], to
        )

    def y_copy(kc):
        return rcopy(S.at[kc, me], S.at[kc, me], ys.at[kc], yr.at[kc], ypart)

    def c_copy(which, kc):
        slot = (me, yme)[which]
        return rcopy(S.at[kc, slot], S.at[kc, slot], cs.at[which, kc], cr.at[which, kc], cpart)

    order = (0, 2, 1, 3)
    acc = jnp.zeros((DB, KI), F32)
    for kc in order:
        for j in range(GO):
            values = feat[pl.ds(kc * GO + j, DB, stride=KO), :]
            acc = acc + values * values
            S[kc, me, j] = values.astype(BF16)
        z_copy(1, kc % 2, kc // 2).start()
        c_copy(0, kc).start()

    eye = lax.broadcasted_iota(jnp.int32, (DB, KI), 0) == lax.broadcasted_iota(jnp.int32, (DB, KI), 1)
    def as_column(row):
        wide = jnp.where(eye, jnp.broadcast_to(row, (DB, KI)), 0.0)
        return jnp.broadcast_to(jnp.sum(wide, axis=1, keepdims=True), (DB, KI))
    column = jnp.broadcast_to(jnp.sum(acc, axis=1, keepdims=True), (DB, KI))
    row = jnp.sum(jnp.where(eye, column, 0.0), axis=0, keepdims=True)
    sq[...] = jnp.broadcast_to(row, (8, KI))

    def sq_copy(p):
        return rcopy(sq, sqr.at[p - 1], qs.at[p - 1], qr.at[p - 1], dev(z, me, lax.rem(me_l + p, NZ)))
    @pl.loop(1, NZ)
    def _(p):
        sq_copy(p).start()
    for kc in order:
        y_copy(kc).start()
    PP[...] = jnp.zeros_like(PP)
    @pl.when(diagonal)
    def _():
        T[...] = jnp.zeros_like(T)
    def norm_copy(t):
        return rcopy(norm, norms.at[me], ns.at[t], nr.at[me], dev(me_l, t, z))
    def other_slots(act):
        @pl.loop(0, 4)
        def _(t):
            @pl.when(jnp.logical_not(diagonal & (t == me)))
            def _():
                act(t)
    def make_norms():
        @pl.loop(1, NZ)
        def _(p):
            sq_copy(p).wait()
        total = sq[0:1, :]
        for p in range(NZ - 1):
            total = total + sqr[p, 0:1, :]
        norm[...] = jnp.broadcast_to(lax.rsqrt(total + epsilon), (8, KI))
        @pl.when(diagonal)
        def _():
            norms[me] = norm[...]
        other_slots(lambda t: norm_copy(t).start())


    def product(kc, xs, pair):
        right = jnp.concatenate([xs[j] for j in range(GO)], axis=1)
        right = jnp.concatenate([right, jnp.zeros((KI - DB, GO * KI), BF16)], axis=0)
        left = jnp.concatenate(
            [jnp.concatenate([S[kc, 2 * pair + r, j] for j in range(GO)], axis=1) for r in range(2)], axis=0
        )
        res = lax.dot_general(left, right, (((1,), (1,)), ((), ())), preferred_element_type=F32)
        return res.reshape(4, PR, KI)

    def multiply(i, pair):
        h1, sub, direction = i // 4, (i // 2) % 2, i % 2
        PP[2 * h1 + direction, pl.ds(4 * pair, 4)] += product(direction * 2 + sub, R.at[i], pair)

    def multiply_own(kc, pair):
        PP[7, pl.ds(4 * pair, 4)] += product(kc, S.at[kc, me], pair)

    def r_copy(b, to):
        return rcopy(PP.at[b, to], RR.at[b, me_l], rs.at[b, to], rr.at[b, me_l], dev(z, me, to))

    def send_partials(b, pair):
        @pl.loop(0, 4)
        def _(q):
            to = 4 * pair + q
            @pl.when(to != me_l)
            def _():
                r_copy(b, to).start()

    def x_copy(b, pair, to):
        return rcopy(
            PP.at[b, 4 * pair + to], RR.at[b, 4 * pair + x], rs.at[b, 4 * pair + to], rr.at[b, 4 * pair + x],
            dev(z, me, 4 * yh + to),
        )

    def p_copy(b):
        return rcopy(XS.at[b], RY.at[b], ps.at[b], pr.at[b], dev(z, me, 4 * (1 - yh) + x))

    def send_over_x(b, pair):
        @pl.loop(1, 4)
        def _(p):
            x_copy(b, pair, lax.rem(x + p, 4)).start()

    def add_over_x(b, pair):
        total = PP[b, 4 * pair + x]
        for p in range(1, 4):
            slot = 4 * pair + lax.rem(x + p, 4)
            rcopy(PP.at[b, 0], RR.at[b, slot], rs.at[b, 0], rr.at[b, slot], up).wait_recv()
            total = total + RR[b, slot]
        @pl.when(pair == yh)
        def _():
            V[b] = total
        @pl.when(pair != yh)
        def _():
            XS[b] = total
            p_copy(b).start()

    def plane_of(b):
        h = b // 2 + 1
        other = jnp.where(b % 2 == 0, z + NZ - h, z + h)
        return lax.rem(jnp.where(b == 7, z, jnp.where(b == 6, z + 4, other)), NZ)

    def l_copy(b):
        return rcopy(V.at[b], L.at[me, me_l % 2], ls.at[b], lr.at[me, me_l % 2], dev(z, me_l // 2, plane_of(b)))

    def l_copy_self(b):
        return pltpu.make_async_copy(V.at[b], L.at[me, me_l % 2], lr.at[me, me_l % 2])

    def t_copy(b):
        return rcopy(V.at[b], T.at[me_l], ts.at[b], tr.at[me_l], dev(plane_of(b), me, z))

    def send_own(b):
        to_self = self_final & (plane_of(b) == me_l)
        @pl.when(to_self)
        def _():
            l_copy_self(b).start()
        @pl.when(jnp.logical_not(to_self))
        def _():
            l_copy(b).start()

    def add_two_steps(b):
        p_copy(b).wait_recv()
        V[b] = V[b] + RY[b]
        send_own(b)

    def add_up(b):
        total = PP[b, me_l]
        for p in range(1, NZ):
            source = lax.rem(me_l + p, NZ)
            rcopy(PP.at[b, 0], RR.at[b, source], rs.at[b, 0], rr.at[b, source], up).wait_recv()
            total = total + RR[b, source]
        V[b] = total
        send_own(b)
        t_copy(b).start()

    far = (lax.rem(z + NZ - 3, NZ) // 4, lax.rem(z + 3, NZ) // 4)
    arriving = lax.rem(z + 4, NZ) // 4

    def pass_on(tick):
        h, sub = tick // 2 + 1, tick % 2
        for direction in range(2):
            z_copy(h, sub, direction).wait_recv()
            if h < 3:
                z_copy(h + 1, sub, direction).start()
            else:
                @pl.when(far[direction] == sub)
                def _():
                    z_copy(4, sub, direction).start()
        if tick < 4:
            y_copy(order[tick]).wait_recv()
            c_copy(1, order[tick]).start()

    for kc in order:
        c_copy(0, kc).wait_recv()
        multiply_own(kc, yl)
    send_over_x(7, yl)

    pass_on(0)
    pass_on(1)
    @pl.loop(0, 4)
    def _(i):
        multiply(i, yl)
    @pl.loop(0, 2)
    def _(b):
        send_over_x(b, yl)
    make_norms()
    pass_on(2)
    pass_on(3)
    @pl.loop(4, 8)
    def _(i):
        multiply(i, yl)
    @pl.loop(2, 4)
    def _(b):
        send_over_x(b, yl)
    for kc in order:
        c_copy(1, kc).wait_recv()
    for kc in order:
        multiply_own(kc, 1 - yl)
    send_over_x(7, 1 - yl)
    @pl.loop(0, 2)
    def _(h1):
        @pl.loop(0, 4)
        def _(i):
            multiply(4 * h1 + i, 1 - yl)
        send_over_x(2 * h1, 1 - yl)
        send_over_x(2 * h1 + 1, 1 - yl)
    add_over_x(7, yl)
    @pl.loop(0, 4)
    def _(b):
        add_over_x(b, yl)
    pass_on(4)
    @pl.loop(0, 4)
    def _(i):
        multiply(8 + i // 2, i % 2)
    pass_on(5)
    @pl.loop(0, 4)
    def _(i):
        multiply(10 + i // 2, i % 2)
    @pl.loop(0, 4)
    def _(i):
        send_partials(4 + i // 2, i % 2)

    add_over_x(7, 1 - yl)
    @pl.loop(0, 4)
    def _(b):
        add_over_x(b, 1 - yl)
    add_two_steps(7)
    @pl.loop(0, 4)
    def _(b):
        add_two_steps(b)

    for direction in range(2):
        z_copy(4, 0, direction).wait_recv()
    for pair in range(2):
        for direction in range(2):
            PP[6, pl.ds(4 * pair, 4)] += product(direction * 2 + arriving, R.at[12 + direction], pair)
        send_partials(6, pair)
    @pl.loop(0, 4)
    def _(b):
        t_copy(b).start()
    @pl.loop(4, 7)
    def _(b):
        add_up(b)

    for h in range(1, 5):
        for sub in range(2 if h < 4 else 1):
            for direction in range(2):
                z_copy(h, sub, direction).wait_send()
    for kc in range(4):
        y_copy(kc).wait_send()
        c_copy(0, kc).wait_send()
        c_copy(1, kc).wait_send()
    other_slots(lambda t: norm_copy(t).wait_send())
    @pl.loop(0, 8)
    def _(b):
        direct = (b >= 4) & (b < 7)
        @pl.when(direct)
        def _():
            @pl.loop(0, NZ)
            def _(to):
                @pl.when(to != me_l)
                def _():
                    r_copy(b, to).wait_send()
        @pl.when(jnp.logical_not(direct))
        def _():
            @pl.loop(0, NZ)
            def _(i):
                @pl.when(i % 4 != x)
                def _():
                    x_copy(b, i // 4, i % 4).wait_send()
            p_copy(b).wait_send()
        to_self = self_final & (plane_of(b) == me_l)
        @pl.when(jnp.logical_not(to_self))
        def _():
            l_copy(b).wait_send()
        @pl.when(b != 7)
        def _():
            t_copy(b).wait_send()

    def norm_arrived(t):
        rcopy(norm, norms.at[t], ns.at[t], nr.at[t], up).wait_recv()
    other_slots(norm_arrived)
    for t in range(4):
        for half in range(2):
            rcopy(V.at[0], L.at[t, half], ls.at[0], lr.at[t, half], up).wait_recv()
    @pl.when(jnp.logical_not(diagonal))
    def _():
        for g in range(NZ):
            rcopy(V.at[0], T.at[g], ts.at[0], tr.at[g], up).wait_recv()
    own = jnp.concatenate([L[t].reshape(DB, KI)[:, :DB] for t in range(4)], axis=1)
    other = jnp.transpose(T[...].reshape(NZ * PR, KI))[:DB, :]
    rows = as_column(norm[0:1, :])
    rows = jnp.concatenate([rows, rows, rows, rows[:, : 4 * DB - 3 * KI]], axis=1)
    columns = jnp.concatenate([norms[t, 0:1, :DB] for t in range(4)], axis=1)
    columns = jnp.broadcast_to(columns, (DB, 4 * DB))
    out_ref[...] = jnp.where((rows > 0) & (columns > 0), (own + other) * rows * columns, 0.0)


def local(grad_out, acts, lengths):
    grads = grad_out.reshape(DB, KO, SEQ)
    inputs = acts.reshape(DB, SEQ, KI)
    dma = pltpu.SemaphoreType.DMA
    return pl.pallas_call(
        body,
        out_shape=jax.ShapeDtypeStruct((DB, 4 * DB), F32),
        in_specs=[
            pl.BlockSpec(memory_space=pltpu.SMEM),
            pl.BlockSpec(memory_space=pl.ANY),
            pl.BlockSpec(memory_space=pl.ANY),
        ],
        out_specs=pl.BlockSpec(memory_space=pltpu.VMEM),
        scratch_shapes=[
            pltpu.VMEM((DB, KO, SEQ), BF16),
            pltpu.VMEM((DB, SEQ, KI), BF16),
            pltpu.VMEM((DB * KO, KI), F32),
            pltpu.VMEM((4, 4, GO, DB, KI), BF16),
            pltpu.VMEM((14, GO, DB, KI), BF16),
            pltpu.VMEM((8, 8, PR, KI), F32),
            pltpu.VMEM((8, 8, PR, KI), F32),
            pltpu.VMEM((8, PR, KI), F32),
            pltpu.VMEM((8, PR, KI), F32),
            pltpu.VMEM((8, PR, KI), F32),
            pltpu.VMEM((4, 2, PR, KI), F32),
            pltpu.VMEM((8, PR, KI), F32),
            pltpu.VMEM((8, KI), F32),
            pltpu.VMEM((7, 8, KI), F32),
            pltpu.VMEM((8, KI), F32),
            pltpu.VMEM((4, 8, KI), F32),
            dma((2, DB // CH)),
            dma((7,)), dma((7,)),
            dma((4,)), dma((4,)),
            dma((2, 4, 2)), dma((2, 4, 2)),
            dma((4,)), dma((4,)),
            dma((2, 4)), dma((2, 4)),
            dma((8, 8)), dma((8, 8)),
            dma((8,)), dma((8,)),
            dma((8,)), dma((8,)),
            dma((4, 2)), dma((8,)),
        ],
        compiler_params=pltpu.CompilerParams(
            collective_id=0, has_side_effects=True, vmem_limit_bytes=62 * 2**20
        ),
    )(lengths, grads, inputs)


def solution(mesh):
    placed = (P("docs", "layer", None, None), P("docs", "layer", None, None), P("docs"))
    return jax.shard_map(
        local, mesh=mesh, in_specs=placed, out_specs=P("docs", "layer"), check_vma=False
    )
```

```python
import functools

import jax
import jax.numpy as jnp
from jax import lax
from jax.experimental import pallas as pl
from jax.experimental.pallas import tpu as pltpu
from jax.sharding import PartitionSpec as P

epsilon = 1e-06
MESH = pl.DeviceIdType.MESH
F32 = jnp.float32
BF16 = jnp.bfloat16

DB = 112
KO = 32
KI = 128
SEQ = 256
NZ = 8
CH = 16
GO = 8
PR = 56


def body(
    lengths_ref, grad_hbm, acts_hbm, out_ref,
    gbuf, abuf, feat, S, R, PP, RR, XS, RY, V, L, T, sq, sqr, norm, norms,
    in_sem, qs, qr, ns, nr, zs, zr, ys, yr, cs, cr, rs, rr, ps, pr, ls, ts, lr, tr,
):
    d = lax.axis_index("docs")
    me_l = lax.axis_index("layer")
    z, yl, c = d // 4, (d // 2) % 2, d % 2
    yh, x = me_l // 4, me_l % 4
    me = yl * 2 + c
    yme = (1 - yl) * 2 + c

    def dev(zz, slot, ll):
        return (zz * 4 + slot, ll)

    up = dev(lax.rem(z + 1, NZ), me, me_l)
    down = dev(lax.rem(z + NZ - 1, NZ), me, me_l)
    ypart = dev(z, yme, me_l)
    cpart = dev(z, yl * 2 + 1 - c, me_l)
    def owner(piece):
        pair, to = piece // 4, piece % 4
        return 4 * ((pair + to) % 2) + to

    mine = 4 * ((yh + x) % 2) + x
    self_final = (mine // 2) == me
    diagonal = me_l == z

    def rcopy(src, dst, ss, rs_, to):
        return pltpu.make_async_remote_copy(
            src_ref=src, dst_ref=dst, send_sem=ss, recv_sem=rs_, device_id=to, device_id_type=MESH
        )

    chunks = DB // CH
    def in_copies(k):
        rows = pl.ds(k * CH, CH)
        return (
            pltpu.make_async_copy(grad_hbm.at[rows], gbuf.at[rows], in_sem.at[0, k]),
            pltpu.make_async_copy(acts_hbm.at[rows], abuf.at[rows], in_sem.at[1, k]),
        )
    for k in range(chunks):
        for copy in in_copies(k):
            copy.start()

    barrier = pltpu.get_barrier_semaphore()
    def hello(to):
        pl.semaphore_signal(barrier, inc=1, device_id=to, device_id_type=MESH)
    for to in (up, down, ypart, cpart):
        hello(to)
    @pl.loop(1, NZ)
    def _(p):
        hello(dev(z, me, lax.rem(me_l + p, NZ)))
    @pl.loop(0, 8)
    def _(i):
        ll = owner(2 * me + i // 4)
        slot = i % 4
        @pl.when(jnp.logical_not((ll == me_l) & (slot == me)))
        def _():
            hello(dev(z, slot, ll))
    @pl.when(jnp.logical_not(diagonal))
    def _():
        @pl.loop(0, NZ)
        def _(g):
            hello(dev(me_l, me, g))
    @pl.loop(0, 4)
    def _(t):
        @pl.when(jnp.logical_not(diagonal & (t == me)))
        def _():
            hello(dev(me_l, t, z))

    @pl.loop(0, chunks)
    def _(k):
        for copy in in_copies(k):
            copy.wait()
        @pl.loop(0, CH, unroll=CH)
        def _(j):
            doc = k * CH + j
            n = lengths_ref[doc]
            slots = lax.broadcasted_iota(jnp.int32, (KO, SEQ), 1)
            valid = (slots < n).astype(F32).astype(BF16)
            feat[pl.ds(pl.multiple_of(doc * KO, KO), KO), :] = jnp.dot(
                gbuf[doc] * valid, abuf[doc], preferred_element_type=F32
            )

    pl.semaphore_wait(barrier, 4 + 7 + 8 + 7 + 4 - self_final.astype(jnp.int32) - diagonal.astype(jnp.int32))

    def slot_of(h, sub, direction):
        return (h - 1) * 4 + sub * 2 + direction

    def z_copy(h, sub, direction):
        kc = direction * 2 + sub
        src = S.at[kc, me] if h == 1 else R.at[slot_of(h - 1, sub, direction)]
        to = (up, down)[direction]
        if h == 4:
            return rcopy(src, R.at[12 + direction], zs.at[direction, 3, 0], zr.at[direction, 3, 0], to)
        return rcopy(
            src, R.at[slot_of(h, sub, direction)], zs.at[direction, h - 1, sub], zr.at[direction, h - 1, sub], to
        )

    def y_copy(kc):
        return rcopy(S.at[kc, me], S.at[kc, me], ys.at[kc], yr.at[kc], ypart)

    def c_copy(which, kc):
        slot = (me, yme)[which]
        return rcopy(S.at[kc, slot], S.at[kc, slot], cs.at[which, kc], cr.at[which, kc], cpart)

    order = (0, 2, 1, 3)
    acc = jnp.zeros((DB, KI), F32)
    for kc in range(4):
        for j in range(GO):
            values = feat[pl.ds(kc * GO + j, DB, stride=KO), :]
            acc = acc + values * values
            S[kc, me, j] = values.astype(BF16)
        z_copy(1, kc % 2, kc // 2).start()
        y_copy(kc).start()
        c_copy(0, kc).start()

    eye = lax.broadcasted_iota(jnp.int32, (DB, KI), 0) == lax.broadcasted_iota(jnp.int32, (DB, KI), 1)
    def as_column(row):
        wide = jnp.where(eye, jnp.broadcast_to(row, (DB, KI)), 0.0)
        return jnp.broadcast_to(jnp.sum(wide, axis=1, keepdims=True), (DB, KI))
    column = jnp.broadcast_to(jnp.sum(acc, axis=1, keepdims=True), (DB, KI))
    row = jnp.sum(jnp.where(eye, column, 0.0), axis=0, keepdims=True)
    sq[...] = jnp.broadcast_to(row, (8, KI))

    def sq_copy(p):
        return rcopy(sq, sqr.at[p - 1], qs.at[p - 1], qr.at[p - 1], dev(z, me, lax.rem(me_l + p, NZ)))
    @pl.loop(1, NZ)
    def _(p):
        sq_copy(p).start()
    PP[...] = jnp.zeros_like(PP)
    @pl.when(diagonal)
    def _():
        T[...] = jnp.zeros_like(T)
    def norm_copy(t):
        return rcopy(norm, norms.at[me], ns.at[t], nr.at[me], dev(me_l, t, z))
    def other_slots(act):
        @pl.loop(0, 4)
        def _(t):
            @pl.when(jnp.logical_not(diagonal & (t == me)))
            def _():
                act(t)
    def make_norms():
        @pl.loop(1, NZ)
        def _(p):
            sq_copy(p).wait()
        total = sq[0:1, :]
        for p in range(NZ - 1):
            total = total + sqr[p, 0:1, :]
        norm[...] = jnp.broadcast_to(lax.rsqrt(total + epsilon), (8, KI))
        @pl.when(diagonal)
        def _():
            norms[me] = norm[...]
        other_slots(lambda t: norm_copy(t).start())


    def product(kc, xs, pair):
        right = jnp.concatenate([xs[j] for j in range(GO)], axis=1)
        right = jnp.concatenate([right, jnp.zeros((KI - DB, GO * KI), BF16)], axis=0)
        left = jnp.concatenate(
            [jnp.concatenate([S[kc, 2 * pair + r, j] for j in range(GO)], axis=1) for r in range(2)], axis=0
        )
        res = lax.dot_general(left, right, (((1,), (1,)), ((), ())), preferred_element_type=F32)
        return res.reshape(4, PR, KI)

    def product_all(kc, xs):
        right = jnp.concatenate([xs[j] for j in range(GO)], axis=1)
        right = jnp.concatenate([right, jnp.zeros((KI - DB, GO * KI), BF16)], axis=0)
        left = jnp.concatenate(
            [jnp.concatenate([S[kc, r, j] for j in range(GO)], axis=1) for r in range(4)], axis=0
        )
        res = lax.dot_general(left, right, (((1,), (1,)), ((), ())), preferred_element_type=F32)
        return res.reshape(8, PR, KI)

    def multiply_all(i):
        h1, sub, direction = i // 4, (i // 2) % 2, i % 2
        PP[2 * h1 + direction] += product_all(direction * 2 + sub, R.at[i])

    def multiply(i, pair):
        h1, sub, direction = i // 4, (i // 2) % 2, i % 2
        PP[2 * h1 + direction, pl.ds(4 * pair, 4)] += product(direction * 2 + sub, R.at[i], pair)

    def multiply_own(kc, pair):
        PP[7, pl.ds(4 * pair, 4)] += product(kc, S.at[kc, me], pair)

    def r_copy(b, to):
        return rcopy(
            PP.at[b, 4 * ((to // 4 + to) % 2) + to % 4], RR.at[b, me_l], rs.at[b, to], rr.at[b, me_l], dev(z, me, to)
        )

    def send_partials(b, pair):
        @pl.loop(0, 4)
        def _(q):
            to = owner(4 * pair + q)
            @pl.when(to != me_l)
            def _():
                r_copy(b, to).start()

    def x_copy(b, pair, to):
        return rcopy(
            PP.at[b, 4 * pair + to], RR.at[b, 4 * pair + x], rs.at[b, 4 * pair + to], rr.at[b, 4 * pair + x],
            dev(z, me, 4 * yh + to),
        )

    def p_copy(b):
        return rcopy(XS.at[b], RY.at[b], ps.at[b], pr.at[b], dev(z, me, 4 * (1 - yh) + x))

    def send_over_x(b, pair):
        @pl.loop(1, 4)
        def _(p):
            x_copy(b, pair, lax.rem(x + p, 4)).start()

    def add_over_x(b, pair):
        total = PP[b, 4 * pair + x]
        for p in range(1, 4):
            slot = 4 * pair + lax.rem(x + p, 4)
            rcopy(PP.at[b, 0], RR.at[b, slot], rs.at[b, 0], rr.at[b, slot], up).wait_recv()
            total = total + RR[b, slot]
        keep = yh == (pair + x) % 2
        @pl.when(keep)
        def _():
            V[b] = total
        @pl.when(jnp.logical_not(keep))
        def _():
            XS[b] = total
            p_copy(b).start()

    def plane_of(b):
        h = b // 2 + 1
        other = jnp.where(b % 2 == 0, z + NZ - h, z + h)
        return lax.rem(jnp.where(b == 7, z, jnp.where(b == 6, z + 4, other)), NZ)

    def l_copy(b):
        return rcopy(V.at[b], L.at[me, mine % 2], ls.at[b], lr.at[me, mine % 2], dev(z, mine // 2, plane_of(b)))

    def l_copy_self(b):
        return pltpu.make_async_copy(V.at[b], L.at[me, mine % 2], lr.at[me, mine % 2])

    def t_copy(b):
        return rcopy(V.at[b], T.at[mine], ts.at[b], tr.at[mine], dev(plane_of(b), me, z))

    def send_own(b):
        to_self = self_final & (plane_of(b) == me_l)
        @pl.when(to_self)
        def _():
            l_copy_self(b).start()
        @pl.when(jnp.logical_not(to_self))
        def _():
            l_copy(b).start()

    def add_two_steps(b):
        p_copy(b).wait_recv()
        V[b] = V[b] + RY[b]

    def add_up(b):
        total = PP[b, mine]
        for p in range(1, NZ):
            source = lax.rem(me_l + p, NZ)
            rcopy(PP.at[b, 0], RR.at[b, source], rs.at[b, 0], rr.at[b, source], up).wait_recv()
            total = total + RR[b, source]
        V[b] = total
        send_own(b)
        t_copy(b).start()

    far = (lax.rem(z + NZ - 3, NZ) // 4, lax.rem(z + 3, NZ) // 4)
    arriving = lax.rem(z + 4, NZ) // 4

    def pass_on(tick):
        h, sub = tick // 2 + 1, tick % 2
        for direction in range(2):
            z_copy(h, sub, direction).wait_recv()
            if h < 3:
                z_copy(h + 1, sub, direction).start()
            else:
                @pl.when(far[direction] == sub)
                def _():
                    z_copy(4, sub, direction).start()
        if tick < 4:
            y_copy(tick).wait_recv()
            c_copy(1, tick).start()

    for kc in order:
        c_copy(0, kc).wait_recv()
        multiply_own(kc, yl)
    send_over_x(7, yl)

    pass_on(0)
    pass_on(1)
    @pl.loop(0, 4)
    def _(i):
        multiply(i, yl)
    @pl.loop(0, 2)
    def _(b):
        send_over_x(b, yl)
    pass_on(2)
    for kc in range(2):
        c_copy(1, kc).wait_recv()
        multiply(2 * kc, 1 - yl)
    send_over_x(0, 1 - yl)
    pass_on(3)
    @pl.loop(4, 8)
    def _(i):
        multiply(i, yl)
    @pl.loop(2, 4)
    def _(b):
        send_over_x(b, yl)
    @pl.loop(0, 2)
    def _(sub):
        multiply(4 + 2 * sub, 1 - yl)
    send_over_x(2, 1 - yl)
    for kc in range(2, 4):
        c_copy(1, kc).wait_recv()
    @pl.loop(0, 2)
    def _(h1):
        @pl.loop(0, 2)
        def _(sub):
            multiply(4 * h1 + 2 * sub + 1, 1 - yl)
        send_over_x(2 * h1 + 1, 1 - yl)
    for kc in range(4):
        multiply_own(kc, 1 - yl)
    send_over_x(7, 1 - yl)
    make_norms()
    pass_on(4)
    @pl.loop(8, 10)
    def _(i):
        multiply_all(i)
    add_over_x(7, yl)
    @pl.loop(0, 4)
    def _(b):
        add_over_x(b, yl)
    pass_on(5)
    @pl.loop(0, 2)
    def _(i):
        multiply_all(10 + i)
        send_partials(4 + i, 0)
        send_partials(4 + i, 1)

    add_over_x(7, 1 - yl)
    @pl.loop(0, 4)
    def _(b):
        add_over_x(b, 1 - yl)
    add_two_steps(7)
    @pl.loop(0, 4)
    def _(b):
        add_two_steps(b)

    for direction in range(2):
        z_copy(4, 0, direction).wait_recv()
    @pl.loop(0, 2)
    def _(direction):
        PP[6] += product_all(direction * 2 + arriving, R.at[12 + direction])
    send_partials(6, 0)
    send_partials(6, 1)
    for h in range(1, 5):
        for sub in range(2 if h < 4 else 1):
            for direction in range(2):
                z_copy(h, sub, direction).wait_send()
    for kc in range(4):
        y_copy(kc).wait_send()
        c_copy(0, kc).wait_send()
        c_copy(1, kc).wait_send()
    other_slots(lambda t: norm_copy(t).wait_send())
    def norm_arrived(t):
        rcopy(norm, norms.at[t], ns.at[t], nr.at[t], up).wait_recv()
    other_slots(norm_arrived)
    @pl.loop(0, 5)
    def _(i):
        b = jnp.where(i == 4, 7, i)
        @pl.loop(0, NZ)
        def _(to):
            @pl.when(to % 4 != x)
            def _():
                x_copy(b, to // 4, to % 4).wait_send()
        p_copy(b).wait_send()

    @pl.loop(4, 7)
    def _(b):
        add_up(b)
    send_own(7)
    @pl.loop(0, 4)
    def _(b):
        send_own(b)
        t_copy(b).start()

    for t in range(4):
        for half in range(2):
            rcopy(V.at[0], L.at[t, half], ls.at[0], lr.at[t, half], up).wait_recv()
    @pl.when(jnp.logical_not(diagonal))
    def _():
        for g in range(NZ):
            rcopy(V.at[0], T.at[g], ts.at[0], tr.at[g], up).wait_recv()
    own = jnp.concatenate([L[t].reshape(DB, KI)[:, :DB] for t in range(4)], axis=1)
    other = jnp.transpose(T[...].reshape(NZ * PR, KI))[:DB, :]
    rows = as_column(norm[0:1, :])
    rows = jnp.concatenate([rows, rows, rows, rows[:, : 4 * DB - 3 * KI]], axis=1)
    columns = jnp.concatenate([norms[t, 0:1, :DB] for t in range(4)], axis=1)
    columns = jnp.broadcast_to(columns, (DB, 4 * DB))
    out_ref[...] = jnp.where((rows > 0) & (columns > 0), (own + other) * rows * columns, 0.0)

    @pl.loop(0, 8)
    def _(b):
        @pl.when((b >= 4) & (b < 7))
        def _():
            @pl.loop(0, NZ)
            def _(to):
                @pl.when(to != me_l)
                def _():
                    r_copy(b, to).wait_send()
        to_self = self_final & (plane_of(b) == me_l)
        @pl.when(jnp.logical_not(to_self))
        def _():
            l_copy(b).wait_send()
        @pl.when(b != 7)
        def _():
            t_copy(b).wait_send()


def local(grad_out, acts, lengths):
    grads = grad_out.reshape(DB, KO, SEQ)
    inputs = acts.reshape(DB, SEQ, KI)
    dma = pltpu.SemaphoreType.DMA
    return pl.pallas_call(
        body,
        out_shape=jax.ShapeDtypeStruct((DB, 4 * DB), F32),
        in_specs=[
            pl.BlockSpec(memory_space=pltpu.SMEM),
            pl.BlockSpec(memory_space=pl.ANY),
            pl.BlockSpec(memory_space=pl.ANY),
        ],
        out_specs=pl.BlockSpec(memory_space=pltpu.VMEM),
        scratch_shapes=[
            pltpu.VMEM((DB, KO, SEQ), BF16),
            pltpu.VMEM((DB, SEQ, KI), BF16),
            pltpu.VMEM((DB * KO, KI), F32),
            pltpu.VMEM((4, 4, GO, DB, KI), BF16),
            pltpu.VMEM((14, GO, DB, KI), BF16),
            pltpu.VMEM((8, 8, PR, KI), F32),
            pltpu.VMEM((8, 8, PR, KI), F32),
            pltpu.VMEM((8, PR, KI), F32),
            pltpu.VMEM((8, PR, KI), F32),
            pltpu.VMEM((8, PR, KI), F32),
            pltpu.VMEM((4, 2, PR, KI), F32),
            pltpu.VMEM((8, PR, KI), F32),
            pltpu.VMEM((8, KI), F32),
            pltpu.VMEM((7, 8, KI), F32),
            pltpu.VMEM((8, KI), F32),
            pltpu.VMEM((4, 8, KI), F32),
            dma((2, DB // CH)),
            dma((7,)), dma((7,)),
            dma((4,)), dma((4,)),
            dma((2, 4, 2)), dma((2, 4, 2)),
            dma((4,)), dma((4,)),
            dma((2, 4)), dma((2, 4)),
            dma((8, 8)), dma((8, 8)),
            dma((8,)), dma((8,)),
            dma((8,)), dma((8,)),
            dma((4, 2)), dma((8,)),
        ],
        compiler_params=pltpu.CompilerParams(
            collective_id=0, has_side_effects=True, vmem_limit_bytes=62 * 2**20
        ),
    )(lengths, grads, inputs)


def solution(mesh):
    placed = (P("docs", "layer", None, None), P("docs", "layer", None, None), P("docs"))
    return jax.shard_map(
        local, mesh=mesh, in_specs=placed, out_specs=P("docs", "layer"), check_vma=False
    )
```

```python
import functools

import jax
import jax.numpy as jnp
from jax import lax
from jax.experimental import pallas as pl
from jax.experimental.pallas import tpu as pltpu
from jax.sharding import PartitionSpec as P

epsilon = 1e-06
MESH = pl.DeviceIdType.MESH
F32 = jnp.float32
BF16 = jnp.bfloat16

DB = 112
KO = 32
KI = 128
SEQ = 256
NZ = 8
CH = 16
GO = 8
PR = 56


def body(
    lengths_ref, grad_hbm, acts_hbm, out_ref,
    gbuf, abuf, feat, S, R, PP, RR, XS, RY, RH, V, L, T, sq, sqr, norm, norms,
    in_sem, qs, qr, ns, nr, zs, zr, ys, yr, cs, cr, rs, rr, ps, pr, hs, hr, ls, ts, lr, tr,
):
    d = lax.axis_index("docs")
    me_l = lax.axis_index("layer")
    z, yl, c = d // 4, (d // 2) % 2, d % 2
    yh, x = me_l // 4, me_l % 4
    me = yl * 2 + c
    yme = (1 - yl) * 2 + c

    def dev(zz, slot, ll):
        return (zz * 4 + slot, ll)

    up = dev(lax.rem(z + 1, NZ), me, me_l)
    down = dev(lax.rem(z + NZ - 1, NZ), me, me_l)
    ypart = dev(z, yme, me_l)
    cpart = dev(z, yl * 2 + 1 - c, me_l)
    def owner(piece):
        pair, to = piece // 4, piece % 4
        return 4 * ((pair + to) % 2) + to

    my_pair = (yh + x) % 2
    mine = 4 * my_pair + x
    self_final = (mine // 2) == me
    diagonal = me_l == z

    def rcopy(src, dst, ss, rs_, to):
        return pltpu.make_async_remote_copy(
            src_ref=src, dst_ref=dst, send_sem=ss, recv_sem=rs_, device_id=to, device_id_type=MESH
        )

    chunks = DB // CH
    def in_copies(k):
        rows = pl.ds(k * CH, CH)
        return (
            pltpu.make_async_copy(grad_hbm.at[rows], gbuf.at[rows], in_sem.at[0, k]),
            pltpu.make_async_copy(acts_hbm.at[rows], abuf.at[rows], in_sem.at[1, k]),
        )
    for k in range(chunks):
        for copy in in_copies(k):
            copy.start()

    barrier = pltpu.get_barrier_semaphore()
    def hello(to):
        pl.semaphore_signal(barrier, inc=1, device_id=to, device_id_type=MESH)
    for to in (up, down, ypart, cpart):
        hello(to)
    @pl.loop(1, NZ)
    def _(p):
        hello(dev(z, me, lax.rem(me_l + p, NZ)))
    @pl.loop(0, 8)
    def _(i):
        ll = owner(2 * me + i // 4)
        slot = i % 4
        @pl.when(jnp.logical_not((ll == me_l) & (slot == me)))
        def _():
            hello(dev(z, slot, ll))
    @pl.when(jnp.logical_not(diagonal))
    def _():
        @pl.loop(0, NZ)
        def _(g):
            hello(dev(me_l, me, g))
    @pl.loop(0, 4)
    def _(t):
        @pl.when(jnp.logical_not(diagonal & (t == me)))
        def _():
            hello(dev(me_l, t, z))

    @pl.loop(0, chunks)
    def _(k):
        for copy in in_copies(k):
            copy.wait()
        @pl.loop(0, CH, unroll=CH)
        def _(j):
            doc = k * CH + j
            n = lengths_ref[doc]
            slots = lax.broadcasted_iota(jnp.int32, (KO, SEQ), 1)
            valid = (slots < n).astype(F32).astype(BF16)
            feat[pl.ds(pl.multiple_of(doc * KO, KO), KO), :] = jnp.dot(
                gbuf[doc] * valid, abuf[doc], preferred_element_type=F32
            )

    pl.semaphore_wait(barrier, 4 + 7 + 8 + 7 + 4 - self_final.astype(jnp.int32) - diagonal.astype(jnp.int32))

    def slot_of(h, sub, direction):
        return (h - 1) * 4 + sub * 2 + direction

    def z_copy(h, sub, direction):
        kc = direction * 2 + sub
        src = S.at[kc, me] if h == 1 else R.at[slot_of(h - 1, sub, direction)]
        to = (up, down)[direction]
        if h == 4:
            return rcopy(src, R.at[12 + direction], zs.at[direction, 3, 0], zr.at[direction, 3, 0], to)
        return rcopy(
            src, R.at[slot_of(h, sub, direction)], zs.at[direction, h - 1, sub], zr.at[direction, h - 1, sub], to
        )

    def y_copy(kc):
        return rcopy(S.at[kc, me], S.at[kc, me], ys.at[kc], yr.at[kc], ypart)

    def c_copy(which, kc):
        slot = (me, yme)[which]
        return rcopy(S.at[kc, slot], S.at[kc, slot], cs.at[which, kc], cr.at[which, kc], cpart)

    order = (0, 2, 1, 3)
    acc = jnp.zeros((DB, KI), F32)
    for i, kc in enumerate(order):
        for j in range(GO):
            values = feat[pl.ds(kc * GO + j, DB, stride=KO), :]
            acc = acc + values * values
            S[kc, me, j] = values.astype(BF16)
        z_copy(1, kc % 2, kc // 2).start()
        c_copy(0, kc).start()
        if i == 1:
            y_copy(0).start()
        if i == 2:
            y_copy(1).start()
            y_copy(2).start()
        if i == 3:
            y_copy(3).start()

    eye = lax.broadcasted_iota(jnp.int32, (DB, KI), 0) == lax.broadcasted_iota(jnp.int32, (DB, KI), 1)
    def as_column(row):
        wide = jnp.where(eye, jnp.broadcast_to(row, (DB, KI)), 0.0)
        return jnp.broadcast_to(jnp.sum(wide, axis=1, keepdims=True), (DB, KI))
    column = jnp.broadcast_to(jnp.sum(acc, axis=1, keepdims=True), (DB, KI))
    row = jnp.sum(jnp.where(eye, column, 0.0), axis=0, keepdims=True)
    sq[...] = jnp.broadcast_to(row, (8, KI))

    def sq_copy(p):
        return rcopy(sq, sqr.at[p - 1], qs.at[p - 1], qr.at[p - 1], dev(z, me, lax.rem(me_l + p, NZ)))
    @pl.loop(1, NZ)
    def _(p):
        sq_copy(p).start()
    PP[...] = jnp.zeros_like(PP)
    @pl.when(diagonal)
    def _():
        T[...] = jnp.zeros_like(T)
    def norm_copy(t):
        return rcopy(norm, norms.at[me], ns.at[t], nr.at[me], dev(me_l, t, z))
    def other_slots(act):
        @pl.loop(0, 4)
        def _(t):
            @pl.when(jnp.logical_not(diagonal & (t == me)))
            def _():
                act(t)
    def make_norms():
        @pl.loop(1, NZ)
        def _(p):
            sq_copy(p).wait()
        total = sq[0:1, :]
        for p in range(NZ - 1):
            total = total + sqr[p, 0:1, :]
        norm[...] = jnp.broadcast_to(lax.rsqrt(total + epsilon), (8, KI))
        @pl.when(diagonal)
        def _():
            norms[me] = norm[...]
        other_slots(lambda t: norm_copy(t).start())


    def product(kc, xs, pair):
        right = jnp.concatenate([xs[j] for j in range(GO)], axis=1)
        right = jnp.concatenate([right, jnp.zeros((KI - DB, GO * KI), BF16)], axis=0)
        left = jnp.concatenate(
            [jnp.concatenate([S[kc, 2 * pair + r, j] for j in range(GO)], axis=1) for r in range(2)], axis=0
        )
        res = lax.dot_general(left, right, (((1,), (1,)), ((), ())), preferred_element_type=F32)
        return res.reshape(4, PR, KI)

    def product_all(kc, xs):
        right = jnp.concatenate([xs[j] for j in range(GO)], axis=1)
        right = jnp.concatenate([right, jnp.zeros((KI - DB, GO * KI), BF16)], axis=0)
        left = jnp.concatenate(
            [jnp.concatenate([S[kc, r, j] for j in range(GO)], axis=1) for r in range(4)], axis=0
        )
        res = lax.dot_general(left, right, (((1,), (1,)), ((), ())), preferred_element_type=F32)
        return res.reshape(8, PR, KI)

    def multiply_all(i):
        h1, sub, direction = i // 4, (i // 2) % 2, i % 2
        PP[2 * h1 + direction] += product_all(direction * 2 + sub, R.at[i])

    def multiply(i, pair):
        h1, sub, direction = i // 4, (i // 2) % 2, i % 2
        PP[2 * h1 + direction, pl.ds(4 * pair, 4)] += product(direction * 2 + sub, R.at[i], pair)

    def multiply_own(kc, pair):
        PP[7, pl.ds(4 * pair, 4)] += product(kc, S.at[kc, me], pair)

    def r_copy(b, to):
        return rcopy(
            PP.at[b, 4 * ((to // 4 + to) % 2) + to % 4], RR.at[b, me_l], rs.at[b, to], rr.at[b, me_l], dev(z, me, to)
        )

    def send_partials(b, pair):
        @pl.loop(0, 4)
        def _(q):
            to = owner(4 * pair + q)
            @pl.when(to != me_l)
            def _():
                r_copy(b, to).start()

    def x_copy(b, pair, to):
        return rcopy(
            PP.at[b, 4 * pair + to], RR.at[b, 4 * pair + x], rs.at[b, 4 * pair + to], rr.at[b, 4 * pair + x],
            dev(z, me, 4 * yh + to),
        )

    def p_copy(b):
        return rcopy(XS.at[b], RY.at[b], ps.at[b], pr.at[b], dev(z, me, 4 * (1 - yh) + x))

    def send_over_x(b, pair):
        @pl.loop(1, 4)
        def _(p):
            x_copy(b, pair, lax.rem(x + p, 4)).start()

    def add_over_x(b, pair):
        total = PP[b, 4 * pair + x]
        for p in range(1, 4):
            slot = 4 * pair + lax.rem(x + p, 4)
            rcopy(PP.at[b, 0], RR.at[b, slot], rs.at[b, 0], rr.at[b, slot], up).wait_recv()
            total = total + RR[b, slot]
        keep = yh == (pair + x) % 2
        @pl.when(keep)
        def _():
            V[b] = total
        @pl.when(jnp.logical_not(keep))
        def _():
            XS[b] = total
            p_copy(b).start()

    def plane_of(b):
        h = b // 2 + 1
        other = jnp.where(b % 2 == 0, z + NZ - h, z + h)
        return lax.rem(jnp.where(b == 7, z, jnp.where(b == 6, z + 4, other)), NZ)

    def l_copy(b):
        return rcopy(V.at[b], L.at[me, mine % 2], ls.at[b], lr.at[me, mine % 2], dev(z, mine // 2, plane_of(b)))

    def l_copy_self(b):
        return pltpu.make_async_copy(V.at[b], L.at[me, mine % 2], lr.at[me, mine % 2])

    def t_copy(b):
        return rcopy(V.at[b], T.at[mine], ts.at[b], tr.at[mine], dev(plane_of(b), me, z))

    def h_copy(b, pair, j):
        piece = 4 * pair + (pair + yh + 1) % 2 + 2 * j
        return rcopy(
            PP.at[b, piece], RH.at[b, pair, j], hs.at[b, pair, j], hr.at[b, pair, j], dev(z, me, 4 * (1 - yh) + x)
        )

    def send_over_y(b, pair):
        for j in range(2):
            h_copy(b, pair, j).start()

    def add_over_y(b, pair):
        for j in range(2):
            to = (pair + yh) % 2 + 2 * j
            h_copy(b, pair, j).wait_recv()
            PP[b, 4 * pair + to] += RH[b, pair, j]
            @pl.when(to != x)
            def _():
                x_copy(b, pair, to).start()

    def over_y_left(b, pair):
        for j in range(2):
            to = (pair + yh) % 2 + 2 * j
            h_copy(b, pair, j).wait_send()
            @pl.when(to != x)
            def _():
                x_copy(b, pair, to).wait_send()

    def over_x_left(b, pair):
        @pl.loop(1, 4)
        def _(p):
            x_copy(b, pair, lax.rem(x + p, 4)).wait_send()
        @pl.when(my_pair != pair)
        def _():
            p_copy(b).wait_send()

    def finish_x(b):
        p_copy(b).wait_recv()
        V[b] = V[b] + RY[b]

    def finish_y(b):
        total = PP[b, mine]
        for p in range(1, 4):
            slot = 4 * my_pair + lax.rem(x + p, 4)
            rcopy(PP.at[b, 0], RR.at[b, slot], rs.at[b, 0], rr.at[b, slot], up).wait_recv()
            total = total + RR[b, slot]
        V[b] = total

    def send_own(b):
        to_self = self_final & (plane_of(b) == me_l)
        @pl.when(to_self)
        def _():
            l_copy_self(b).start()
        @pl.when(jnp.logical_not(to_self))
        def _():
            l_copy(b).start()

    def add_up(b):
        total = PP[b, mine]
        for p in range(1, NZ):
            source = lax.rem(me_l + p, NZ)
            rcopy(PP.at[b, 0], RR.at[b, source], rs.at[b, 0], rr.at[b, source], up).wait_recv()
            total = total + RR[b, source]
        V[b] = total

    far = (lax.rem(z + NZ - 3, NZ) // 4, lax.rem(z + 3, NZ) // 4)
    arriving = lax.rem(z + 4, NZ) // 4

    def pass_on(tick):
        h, sub = tick // 2 + 1, tick % 2
        for direction in range(2):
            z_copy(h, sub, direction).wait_recv()
            if h < 3:
                z_copy(h + 1, sub, direction).start()
            else:
                @pl.when(far[direction] == sub)
                def _():
                    z_copy(4, sub, direction).start()
        if tick < 4:
            y_copy(tick).wait_recv()
            c_copy(1, tick).start()

    for kc in order:
        c_copy(0, kc).wait_recv()
        multiply_own(kc, yl)
    send_over_x(7, yl)

    pass_on(0)
    pass_on(1)
    @pl.loop(0, 4)
    def _(i):
        multiply(i, yl)
    @pl.loop(0, 2)
    def _(b):
        send_over_x(b, yl)
    pass_on(2)
    for kc in range(2):
        c_copy(1, kc).wait_recv()
        multiply(2 * kc, 1 - yl)
    send_over_x(0, 1 - yl)
    pass_on(3)
    @pl.loop(4, 8)
    def _(i):
        multiply(i, yl)
    send_over_y(2, yl)
    send_over_y(3, yl)
    @pl.loop(0, 2)
    def _(sub):
        multiply(4 + 2 * sub, 1 - yl)
    send_over_y(2, 1 - yl)
    for kc in range(2, 4):
        c_copy(1, kc).wait_recv()
    @pl.loop(0, 2)
    def _(h1):
        @pl.loop(0, 2)
        def _(sub):
            multiply(4 * h1 + 2 * sub + 1, 1 - yl)
        @pl.when(h1 == 0)
        def _():
            send_over_x(1, 1 - yl)
        @pl.when(h1 == 1)
        def _():
            send_over_y(3, 1 - yl)
    for kc in range(4):
        multiply_own(kc, 1 - yl)
    send_over_x(7, 1 - yl)
    add_over_x(7, yl)
    add_over_x(0, yl)
    add_over_x(1, yl)
    add_over_x(0, 1 - yl)
    make_norms()
    pass_on(4)
    @pl.loop(8, 10)
    def _(i):
        multiply_all(i)
    add_over_y(2, yl)
    add_over_y(3, yl)
    add_over_y(2, 1 - yl)
    pass_on(5)
    @pl.loop(0, 2)
    def _(i):
        multiply_all(10 + i)
        send_partials(4 + i, 0)
        send_partials(4 + i, 1)
    add_over_y(3, 1 - yl)
    add_over_x(1, 1 - yl)
    add_over_x(7, 1 - yl)

    for direction in range(2):
        z_copy(4, 0, direction).wait_recv()
    @pl.loop(0, 2)
    def _(direction):
        PP[6] += product_all(direction * 2 + arriving, R.at[12 + direction])
    send_partials(6, 0)
    send_partials(6, 1)
    for h in range(1, 5):
        for sub in range(2 if h < 4 else 1):
            for direction in range(2):
                z_copy(h, sub, direction).wait_send()
    for kc in range(4):
        y_copy(kc).wait_send()
        c_copy(0, kc).wait_send()
        c_copy(1, kc).wait_send()
    other_slots(lambda t: norm_copy(t).wait_send())
    def norm_arrived(t):
        rcopy(norm, norms.at[t], ns.at[t], nr.at[t], up).wait_recv()
    other_slots(norm_arrived)
    over_x_left(7, yl)
    over_x_left(0, yl)
    over_x_left(1, yl)
    over_x_left(0, 1 - yl)
    for pair in (yl, 1 - yl):
        over_y_left(2, pair)
        over_y_left(3, pair)
    over_x_left(1, 1 - yl)
    over_x_left(7, 1 - yl)

    finish_x(0)
    finish_x(1)
    finish_y(2)
    finish_y(3)
    finish_x(7)
    @pl.loop(4, 6)
    def _(b):
        add_up(b)
    add_up(6)
    t_copy(6).start()
    send_own(6)
    @pl.loop(4, 6)
    def _(b):
        t_copy(b).start()
        send_own(b)
    @pl.loop(0, 4)
    def _(b):
        t_copy(b).start()
    send_own(7)
    @pl.loop(0, 4)
    def _(b):
        send_own(b)

    @pl.loop(0, 8)
    def _(b):
        @pl.when((b >= 4) & (b < 7))
        def _():
            @pl.loop(0, NZ)
            def _(to):
                @pl.when(to != me_l)
                def _():
                    r_copy(b, to).wait_send()
        to_self = self_final & (plane_of(b) == me_l)
        @pl.when(jnp.logical_not(to_self))
        def _():
            l_copy(b).wait_send()
        @pl.when(b != 7)
        def _():
            t_copy(b).wait_send()

    for t in range(4):
        for half in range(2):
            rcopy(V.at[0], L.at[t, half], ls.at[0], lr.at[t, half], up).wait_recv()
    @pl.when(jnp.logical_not(diagonal))
    def _():
        for g in range(NZ):
            rcopy(V.at[0], T.at[g], ts.at[0], tr.at[g], up).wait_recv()
    own = jnp.concatenate([L[t].reshape(DB, KI)[:, :DB] for t in range(4)], axis=1)
    other = jnp.transpose(T[...].reshape(NZ * PR, KI))[:DB, :]
    rows = as_column(norm[0:1, :])
    rows = jnp.concatenate([rows, rows, rows, rows[:, : 4 * DB - 3 * KI]], axis=1)
    columns = jnp.concatenate([norms[t, 0:1, :DB] for t in range(4)], axis=1)
    columns = jnp.broadcast_to(columns, (DB, 4 * DB))
    out_ref[...] = jnp.where((rows > 0) & (columns > 0), (own + other) * rows * columns, 0.0)


def local(grad_out, acts, lengths):
    grads = grad_out.reshape(DB, KO, SEQ)
    inputs = acts.reshape(DB, SEQ, KI)
    dma = pltpu.SemaphoreType.DMA
    return pl.pallas_call(
        body,
        out_shape=jax.ShapeDtypeStruct((DB, 4 * DB), F32),
        in_specs=[
            pl.BlockSpec(memory_space=pltpu.SMEM),
            pl.BlockSpec(memory_space=pl.ANY),
            pl.BlockSpec(memory_space=pl.ANY),
        ],
        out_specs=pl.BlockSpec(memory_space=pltpu.VMEM),
        scratch_shapes=[
            pltpu.VMEM((DB, KO, SEQ), BF16),
            pltpu.VMEM((DB, SEQ, KI), BF16),
            pltpu.VMEM((DB * KO, KI), F32),
            pltpu.VMEM((4, 4, GO, DB, KI), BF16),
            pltpu.VMEM((14, GO, DB, KI), BF16),
            pltpu.VMEM((8, 8, PR, KI), F32),
            pltpu.VMEM((8, 8, PR, KI), F32),
            pltpu.VMEM((8, PR, KI), F32),
            pltpu.VMEM((8, PR, KI), F32),
            pltpu.VMEM((8, 2, 2, PR, KI), F32),
            pltpu.VMEM((8, PR, KI), F32),
            pltpu.VMEM((4, 2, PR, KI), F32),
            pltpu.VMEM((8, PR, KI), F32),
            pltpu.VMEM((8, KI), F32),
            pltpu.VMEM((7, 8, KI), F32),
            pltpu.VMEM((8, KI), F32),
            pltpu.VMEM((4, 8, KI), F32),
            dma((2, DB // CH)),
            dma((7,)), dma((7,)),
            dma((4,)), dma((4,)),
            dma((2, 4, 2)), dma((2, 4, 2)),
            dma((4,)), dma((4,)),
            dma((2, 4)), dma((2, 4)),
            dma((8, 8)), dma((8, 8)),
            dma((8,)), dma((8,)),
            dma((8, 2, 2)), dma((8, 2, 2)),
            dma((8,)), dma((8,)),
            dma((4, 2)), dma((8,)),
        ],
        compiler_params=pltpu.CompilerParams(
            collective_id=0, has_side_effects=True, vmem_limit_bytes=62 * 2**20
        ),
    )(lengths, grads, inputs)


def solution(mesh):
    placed = (P("docs", "layer", None, None), P("docs", "layer", None, None), P("docs"))
    return jax.shard_map(
        local, mesh=mesh, in_specs=placed, out_specs=P("docs", "layer"), check_vma=False
    )
```

```python
import functools

import jax
import jax.numpy as jnp
from jax import lax
from jax.experimental import pallas as pl
from jax.experimental.pallas import tpu as pltpu
from jax.sharding import PartitionSpec as P

epsilon = 1e-06
MESH = pl.DeviceIdType.MESH
F32 = jnp.float32
BF16 = jnp.bfloat16

DB = 112
KO = 32
KI = 128
SEQ = 256
NZ = 8
CH = 16
GO = 8
PR = 56


def body(
    lengths_ref, grad_hbm, acts_hbm, out_ref,
    gbuf, abuf, feat, S, R, PP, RR, XS, RY, RH, V, L, T, sq, sqr, norm, norms,
    in_sem, qs, qr, ns, nr, zs, zr, ys, yr, cs, cr, rs, rr, ps, pr, hs, hr, ls, ts, lr, tr,
):
    d = lax.axis_index("docs")
    me_l = lax.axis_index("layer")
    z, yl, c = d // 4, (d // 2) % 2, d % 2
    yh, x = me_l // 4, me_l % 4
    me = yl * 2 + c
    yme = (1 - yl) * 2 + c

    def dev(zz, slot, ll):
        return (zz * 4 + slot, ll)

    up = dev(lax.rem(z + 1, NZ), me, me_l)
    down = dev(lax.rem(z + NZ - 1, NZ), me, me_l)
    ypart = dev(z, yme, me_l)
    cpart = dev(z, yl * 2 + 1 - c, me_l)
    def owner(piece):
        pair, to = piece // 4, piece % 4
        return 4 * ((pair + to) % 2) + to

    my_pair = (yh + x) % 2
    mine = 4 * my_pair + x
    self_final = (mine // 2) == me
    diagonal = me_l == z

    def rcopy(src, dst, ss, rs_, to):
        return pltpu.make_async_remote_copy(
            src_ref=src, dst_ref=dst, send_sem=ss, recv_sem=rs_, device_id=to, device_id_type=MESH
        )

    chunks = DB // CH
    def in_copies(k):
        rows = pl.ds(k * CH, CH)
        return (
            pltpu.make_async_copy(grad_hbm.at[rows], gbuf.at[rows], in_sem.at[0, k]),
            pltpu.make_async_copy(acts_hbm.at[rows], abuf.at[rows], in_sem.at[1, k]),
        )
    for k in range(chunks):
        for copy in in_copies(k):
            copy.start()

    barrier = pltpu.get_barrier_semaphore()
    def hello(to):
        pl.semaphore_signal(barrier, inc=1, device_id=to, device_id_type=MESH)
    for to in (up, down, ypart, cpart):
        hello(to)
    @pl.loop(1, NZ)
    def _(p):
        hello(dev(z, me, lax.rem(me_l + p, NZ)))
    @pl.loop(0, 8)
    def _(i):
        ll = owner(2 * me + i // 4)
        slot = i % 4
        @pl.when(jnp.logical_not((ll == me_l) & (slot == me)))
        def _():
            hello(dev(z, slot, ll))
    @pl.when(jnp.logical_not(diagonal))
    def _():
        @pl.loop(0, NZ)
        def _(g):
            hello(dev(me_l, me, g))
    @pl.loop(0, 4)
    def _(t):
        @pl.when(jnp.logical_not(diagonal & (t == me)))
        def _():
            hello(dev(me_l, t, z))

    @pl.loop(0, chunks)
    def _(k):
        for copy in in_copies(k):
            copy.wait()
        @pl.loop(0, CH, unroll=CH)
        def _(j):
            doc = k * CH + j
            n = lengths_ref[doc]
            slots = lax.broadcasted_iota(jnp.int32, (KO, SEQ), 1)
            valid = (slots < n).astype(F32).astype(BF16)
            feat[pl.ds(pl.multiple_of(doc * KO, KO), KO), :] = jnp.dot(
                gbuf[doc] * valid, abuf[doc], preferred_element_type=F32
            )

    pl.semaphore_wait(barrier, 4 + 7 + 8 + 7 + 4 - self_final.astype(jnp.int32) - diagonal.astype(jnp.int32))

    def slot_of(h, sub, direction):
        return (h - 1) * 4 + sub * 2 + direction

    def z_copy(h, sub, direction):
        kc = direction * 2 + sub
        src = S.at[kc, me] if h == 1 else R.at[slot_of(h - 1, sub, direction)]
        to = (up, down)[direction]
        if h == 4:
            return rcopy(src, R.at[12 + direction], zs.at[direction, 3, 0], zr.at[direction, 3, 0], to)
        return rcopy(
            src, R.at[slot_of(h, sub, direction)], zs.at[direction, h - 1, sub], zr.at[direction, h - 1, sub], to
        )

    def y_copy(kc):
        return rcopy(S.at[kc, me], S.at[kc, me], ys.at[kc], yr.at[kc], ypart)

    def c_copy(which, kc):
        slot = (me, yme)[which]
        return rcopy(S.at[kc, slot], S.at[kc, slot], cs.at[which, kc], cr.at[which, kc], cpart)

    order = (0, 2, 1, 3)
    acc = jnp.zeros((DB, KI), F32)
    for i, kc in enumerate(order):
        for j in range(GO):
            values = feat[pl.ds(kc * GO + j, DB, stride=KO), :]
            acc = acc + values * values
            S[kc, me, j] = values.astype(BF16)
        z_copy(1, kc % 2, kc // 2).start()
        c_copy(0, kc).start()
        if i == 1:
            y_copy(0).start()
        if i == 2:
            y_copy(1).start()
            y_copy(2).start()
        if i == 3:
            y_copy(3).start()

    eye = lax.broadcasted_iota(jnp.int32, (DB, KI), 0) == lax.broadcasted_iota(jnp.int32, (DB, KI), 1)
    def as_column(row):
        wide = jnp.where(eye, jnp.broadcast_to(row, (DB, KI)), 0.0)
        return jnp.broadcast_to(jnp.sum(wide, axis=1, keepdims=True), (DB, KI))
    column = jnp.broadcast_to(jnp.sum(acc, axis=1, keepdims=True), (DB, KI))
    row = jnp.sum(jnp.where(eye, column, 0.0), axis=0, keepdims=True)
    sq[...] = jnp.broadcast_to(row, (8, KI))

    def sq_copy(p):
        return rcopy(sq, sqr.at[p - 1], qs.at[p - 1], qr.at[p - 1], dev(z, me, lax.rem(me_l + p, NZ)))
    @pl.loop(1, NZ)
    def _(p):
        sq_copy(p).start()
    PP[...] = jnp.zeros_like(PP)
    @pl.when(diagonal)
    def _():
        T[...] = jnp.zeros_like(T)
    def norm_copy(t):
        return rcopy(norm, norms.at[me], ns.at[t], nr.at[me], dev(me_l, t, z))
    def other_slots(act):
        @pl.loop(0, 4)
        def _(t):
            @pl.when(jnp.logical_not(diagonal & (t == me)))
            def _():
                act(t)
    def make_norms():
        @pl.loop(1, NZ)
        def _(p):
            sq_copy(p).wait()
        total = sq[0:1, :]
        for p in range(NZ - 1):
            total = total + sqr[p, 0:1, :]
        norm[...] = jnp.broadcast_to(lax.rsqrt(total + epsilon), (8, KI))
        @pl.when(diagonal)
        def _():
            norms[me] = norm[...]
        other_slots(lambda t: norm_copy(t).start())


    def product(kc, xs, pair):
        right = jnp.concatenate([xs[j] for j in range(GO)], axis=1)
        right = jnp.concatenate([right, jnp.zeros((KI - DB, GO * KI), BF16)], axis=0)
        left = jnp.concatenate(
            [jnp.concatenate([S[kc, 2 * pair + r, j] for j in range(GO)], axis=1) for r in range(2)], axis=0
        )
        res = lax.dot_general(left, right, (((1,), (1,)), ((), ())), preferred_element_type=F32)
        return res.reshape(4, PR, KI)

    def product_all(kc, xs):
        right = jnp.concatenate([xs[j] for j in range(GO)], axis=1)
        right = jnp.concatenate([right, jnp.zeros((KI - DB, GO * KI), BF16)], axis=0)
        left = jnp.concatenate(
            [jnp.concatenate([S[kc, r, j] for j in range(GO)], axis=1) for r in range(4)], axis=0
        )
        res = lax.dot_general(left, right, (((1,), (1,)), ((), ())), preferred_element_type=F32)
        return res.reshape(8, PR, KI)

    def multiply_all(i):
        h1, sub, direction = i // 4, (i // 2) % 2, i % 2
        PP[2 * h1 + direction] += product_all(direction * 2 + sub, R.at[i])

    def multiply(i, pair):
        h1, sub, direction = i // 4, (i // 2) % 2, i % 2
        PP[2 * h1 + direction, pl.ds(4 * pair, 4)] += product(direction * 2 + sub, R.at[i], pair)

    def multiply_own(kc, pair):
        PP[7, pl.ds(4 * pair, 4)] += product(kc, S.at[kc, me], pair)

    def r_copy(b, to):
        return rcopy(
            PP.at[b, 4 * ((to // 4 + to) % 2) + to % 4], RR.at[b, me_l], rs.at[b, to], rr.at[b, me_l], dev(z, me, to)
        )

    def send_partials(b, pair):
        @pl.loop(0, 4)
        def _(q):
            to = owner(4 * pair + q)
            @pl.when(to != me_l)
            def _():
                r_copy(b, to).start()

    def x_copy(b, pair, to):
        return rcopy(
            PP.at[b, 4 * pair + to], RR.at[b, 4 * pair + x], rs.at[b, 4 * pair + to], rr.at[b, 4 * pair + x],
            dev(z, me, 4 * yh + to),
        )

    def p_copy(b):
        return rcopy(XS.at[b], RY.at[b], ps.at[b], pr.at[b], dev(z, me, 4 * (1 - yh) + x))

    def send_over_x(b, pair):
        @pl.loop(1, 4)
        def _(p):
            x_copy(b, pair, lax.rem(x + p, 4)).start()

    def add_over_x(b, pair):
        total = PP[b, 4 * pair + x]
        for p in range(1, 4):
            slot = 4 * pair + lax.rem(x + p, 4)
            rcopy(PP.at[b, 0], RR.at[b, slot], rs.at[b, 0], rr.at[b, slot], up).wait_recv()
            total = total + RR[b, slot]
        keep = yh == (pair + x) % 2
        @pl.when(keep)
        def _():
            V[b] = total
        @pl.when(jnp.logical_not(keep))
        def _():
            XS[b] = total
            p_copy(b).start()

    def plane_of(b):
        h = b // 2 + 1
        other = jnp.where(b % 2 == 0, z + NZ - h, z + h)
        return lax.rem(jnp.where(b == 7, z, jnp.where(b == 6, z + 4, other)), NZ)

    def l_copy(b):
        return rcopy(V.at[b], L.at[me, mine % 2], ls.at[b], lr.at[me, mine % 2], dev(z, mine // 2, plane_of(b)))

    def l_copy_self(b):
        return pltpu.make_async_copy(V.at[b], L.at[me, mine % 2], lr.at[me, mine % 2])

    def t_copy(b):
        return rcopy(V.at[b], T.at[mine], ts.at[b], tr.at[mine], dev(plane_of(b), me, z))

    def h_copy(b, pair, j):
        piece = 4 * pair + (pair + yh + 1) % 2 + 2 * j
        return rcopy(
            PP.at[b, piece], RH.at[b, pair, j], hs.at[b, pair, j], hr.at[b, pair, j], dev(z, me, 4 * (1 - yh) + x)
        )

    def send_over_y(b, pair):
        for j in range(2):
            h_copy(b, pair, j).start()

    def add_over_y(b, pair):
        for j in range(2):
            to = (pair + yh) % 2 + 2 * j
            h_copy(b, pair, j).wait_recv()
            PP[b, 4 * pair + to] += RH[b, pair, j]
            @pl.when(to != x)
            def _():
                x_copy(b, pair, to).start()

    def over_y_left(b, pair):
        for j in range(2):
            to = (pair + yh) % 2 + 2 * j
            h_copy(b, pair, j).wait_send()
            @pl.when(to != x)
            def _():
                x_copy(b, pair, to).wait_send()

    def over_x_left(b, pair):
        @pl.loop(1, 4)
        def _(p):
            x_copy(b, pair, lax.rem(x + p, 4)).wait_send()
        @pl.when(my_pair != pair)
        def _():
            p_copy(b).wait_send()

    def finish_x(b):
        p_copy(b).wait_recv()
        V[b] = V[b] + RY[b]

    def finish_y(b):
        total = PP[b, mine]
        for p in range(1, 4):
            slot = 4 * my_pair + lax.rem(x + p, 4)
            rcopy(PP.at[b, 0], RR.at[b, slot], rs.at[b, 0], rr.at[b, slot], up).wait_recv()
            total = total + RR[b, slot]
        V[b] = total

    def send_own(b):
        to_self = self_final & (plane_of(b) == me_l)
        @pl.when(to_self)
        def _():
            l_copy_self(b).start()
        @pl.when(jnp.logical_not(to_self))
        def _():
            l_copy(b).start()

    def add_up(b):
        total = PP[b, mine]
        for p in range(1, NZ):
            source = lax.rem(me_l + p, NZ)
            rcopy(PP.at[b, 0], RR.at[b, source], rs.at[b, 0], rr.at[b, source], up).wait_recv()
            total = total + RR[b, source]
        V[b] = total

    far = (lax.rem(z + NZ - 3, NZ) // 4, lax.rem(z + 3, NZ) // 4)
    arriving = lax.rem(z + 4, NZ) // 4

    def pass_on(tick):
        h, sub = tick // 2 + 1, tick % 2
        for direction in range(2):
            z_copy(h, sub, direction).wait_recv()
            if h < 3:
                z_copy(h + 1, sub, direction).start()
            else:
                @pl.when(far[direction] == sub)
                def _():
                    z_copy(4, sub, direction).start()
        if tick < 4:
            y_copy(tick).wait_recv()
            c_copy(1, tick).start()

    for kc in order:
        c_copy(0, kc).wait_recv()
        multiply_own(kc, yl)
    send_over_x(7, yl)

    pass_on(0)
    pass_on(1)
    @pl.loop(0, 4)
    def _(i):
        multiply(i, yl)
    @pl.loop(0, 2)
    def _(b):
        send_over_x(b, yl)
    pass_on(2)
    for kc in range(2):
        c_copy(1, kc).wait_recv()
        multiply(2 * kc, 1 - yl)
    send_over_x(0, 1 - yl)
    pass_on(3)
    @pl.loop(4, 8)
    def _(i):
        multiply(i, yl)
    send_over_y(2, yl)
    send_over_y(3, yl)
    @pl.loop(0, 2)
    def _(sub):
        multiply(4 + 2 * sub, 1 - yl)
    send_over_y(2, 1 - yl)
    for kc in range(2, 4):
        c_copy(1, kc).wait_recv()
    @pl.loop(0, 2)
    def _(h1):
        @pl.loop(0, 2)
        def _(sub):
            multiply(4 * h1 + 2 * sub + 1, 1 - yl)
        @pl.when(h1 == 0)
        def _():
            send_over_x(1, 1 - yl)
        @pl.when(h1 == 1)
        def _():
            send_over_x(3, 1 - yl)
    for kc in range(4):
        multiply_own(kc, 1 - yl)
    send_over_x(7, 1 - yl)
    add_over_x(7, yl)
    add_over_x(0, yl)
    add_over_x(1, yl)
    add_over_x(0, 1 - yl)
    make_norms()
    pass_on(4)
    @pl.loop(8, 10)
    def _(i):
        multiply_all(i)
    add_over_y(2, yl)
    add_over_y(3, yl)
    add_over_y(2, 1 - yl)
    pass_on(5)
    @pl.loop(0, 2)
    def _(i):
        multiply_all(10 + i)
        send_partials(4 + i, 0)
        send_partials(4 + i, 1)
    add_over_x(3, 1 - yl)
    add_over_x(1, 1 - yl)
    add_over_x(7, 1 - yl)

    for direction in range(2):
        z_copy(4, 0, direction).wait_recv()
    @pl.loop(0, 2)
    def _(direction):
        PP[6] += product_all(direction * 2 + arriving, R.at[12 + direction])
    send_partials(6, 0)
    send_partials(6, 1)
    for h in range(1, 5):
        for sub in range(2 if h < 4 else 1):
            for direction in range(2):
                z_copy(h, sub, direction).wait_send()
    for kc in range(4):
        y_copy(kc).wait_send()
        c_copy(0, kc).wait_send()
        c_copy(1, kc).wait_send()
    other_slots(lambda t: norm_copy(t).wait_send())
    def norm_arrived(t):
        rcopy(norm, norms.at[t], ns.at[t], nr.at[t], up).wait_recv()
    other_slots(norm_arrived)
    over_x_left(7, yl)
    over_x_left(0, yl)
    over_x_left(1, yl)
    over_x_left(0, 1 - yl)
    for pair in (yl, 1 - yl):
        over_y_left(2, pair)
    over_y_left(3, yl)
    over_x_left(3, 1 - yl)
    over_x_left(1, 1 - yl)
    over_x_left(7, 1 - yl)

    finish_x(0)
    finish_x(1)
    finish_y(2)
    @pl.when(my_pair == yl)
    def _():
        finish_y(3)
    @pl.when(my_pair != yl)
    def _():
        finish_x(3)
    finish_x(7)
    @pl.loop(4, 6)
    def _(b):
        add_up(b)
    add_up(6)
    t_copy(6).start()
    send_own(6)
    @pl.loop(4, 6)
    def _(b):
        t_copy(b).start()
        send_own(b)
    @pl.loop(0, 4)
    def _(b):
        t_copy(b).start()
    send_own(7)
    @pl.loop(0, 4)
    def _(b):
        send_own(b)

    @pl.loop(0, 8)
    def _(b):
        @pl.when((b >= 4) & (b < 7))
        def _():
            @pl.loop(0, NZ)
            def _(to):
                @pl.when(to != me_l)
                def _():
                    r_copy(b, to).wait_send()
        to_self = self_final & (plane_of(b) == me_l)
        @pl.when(jnp.logical_not(to_self))
        def _():
            l_copy(b).wait_send()
        @pl.when(b != 7)
        def _():
            t_copy(b).wait_send()

    for t in range(4):
        for half in range(2):
            rcopy(V.at[0], L.at[t, half], ls.at[0], lr.at[t, half], up).wait_recv()
    @pl.when(jnp.logical_not(diagonal))
    def _():
        for g in range(NZ):
            rcopy(V.at[0], T.at[g], ts.at[0], tr.at[g], up).wait_recv()
    own = jnp.concatenate([L[t].reshape(DB, KI)[:, :DB] for t in range(4)], axis=1)
    other = jnp.transpose(T[...].reshape(NZ * PR, KI))[:DB, :]
    rows = as_column(norm[0:1, :])
    rows = jnp.concatenate([rows, rows, rows, rows[:, : 4 * DB - 3 * KI]], axis=1)
    columns = jnp.concatenate([norms[t, 0:1, :DB] for t in range(4)], axis=1)
    columns = jnp.broadcast_to(columns, (DB, 4 * DB))
    out_ref[...] = jnp.where((rows > 0) & (columns > 0), (own + other) * rows * columns, 0.0)


def local(grad_out, acts, lengths):
    grads = grad_out.reshape(DB, KO, SEQ)
    inputs = acts.reshape(DB, SEQ, KI)
    dma = pltpu.SemaphoreType.DMA
    return pl.pallas_call(
        body,
        out_shape=jax.ShapeDtypeStruct((DB, 4 * DB), F32),
        in_specs=[
            pl.BlockSpec(memory_space=pltpu.SMEM),
            pl.BlockSpec(memory_space=pl.ANY),
            pl.BlockSpec(memory_space=pl.ANY),
        ],
        out_specs=pl.BlockSpec(memory_space=pltpu.VMEM),
        scratch_shapes=[
            pltpu.VMEM((DB, KO, SEQ), BF16),
            pltpu.VMEM((DB, SEQ, KI), BF16),
            pltpu.VMEM((DB * KO, KI), F32),
            pltpu.VMEM((4, 4, GO, DB, KI), BF16),
            pltpu.VMEM((14, GO, DB, KI), BF16),
            pltpu.VMEM((8, 8, PR, KI), F32),
            pltpu.VMEM((8, 8, PR, KI), F32),
            pltpu.VMEM((8, PR, KI), F32),
            pltpu.VMEM((8, PR, KI), F32),
            pltpu.VMEM((8, 2, 2, PR, KI), F32),
            pltpu.VMEM((8, PR, KI), F32),
            pltpu.VMEM((4, 2, PR, KI), F32),
            pltpu.VMEM((8, PR, KI), F32),
            pltpu.VMEM((8, KI), F32),
            pltpu.VMEM((7, 8, KI), F32),
            pltpu.VMEM((8, KI), F32),
            pltpu.VMEM((4, 8, KI), F32),
            dma((2, DB // CH)),
            dma((7,)), dma((7,)),
            dma((4,)), dma((4,)),
            dma((2, 4, 2)), dma((2, 4, 2)),
            dma((4,)), dma((4,)),
            dma((2, 4)), dma((2, 4)),
            dma((8, 8)), dma((8, 8)),
            dma((8,)), dma((8,)),
            dma((8, 2, 2)), dma((8, 2, 2)),
            dma((8,)), dma((8,)),
            dma((4, 2)), dma((8,)),
        ],
        compiler_params=pltpu.CompilerParams(
            collective_id=0, has_side_effects=True, vmem_limit_bytes=62 * 2**20
        ),
    )(lengths, grads, inputs)


def solution(mesh):
    placed = (P("docs", "layer", None, None), P("docs", "layer", None, None), P("docs"))
    return jax.shard_map(
        local, mesh=mesh, in_specs=placed, out_specs=P("docs", "layer"), check_vma=False
    )
```
